512 devices in a mesh: seq: 64 (over x_hi, z, core), head: 8 (over x_lo, y).
Axes of the slice: x: 4 (x_hi: 2, x_lo: 2; x = x_hi * 2 + x_lo), y: 4, z: 16, core: 2. Of those that a mesh axis runs over, the one named last changes fastest.
Arguments:
- queries: bfloat16 [32768, 4096], P(('seq', 'head')), may hold values from -5 to 5
- keys: bfloat16 [32768, 1024], P(('seq', 'head')), may hold values from -5 to 5
- values: bfloat16 [32768, 1024], P(('seq', 'head')), may hold values from -5 to 5
- upstream: bfloat16 [32768, 4096], P('seq', 'head'), may hold values from -786432 to 786432
- loss_mask: int32 [32768], P('seq'), may hold values 0 or 1
- parents: int32 [64], replicated, may hold values from -1 to 62, as said below
- token_count: int32 [1], replicated, may hold values from 8192 to 32768
Outputs:
- attended: bfloat16 [32768, 4096], P('seq', 'head')
- query_gradient: bfloat16 [32768, 4096], P('seq', 'head')
- key_gradient: bfloat16 [32768, 1024], P('seq', 'head')
- value_gradient: bfloat16 [32768, 1024], P('seq', 'head')
The draws below stay inside these ranges and needn't reach their ends.
Inputs may be any that keep to these rules, and one draw needn't show every extreme that they name: A rollout tree is a run of at most 3 consecutive segments; parents[g] is -1 for its first segment and otherwise an earlier segment of the same tree, so every ancestor of g lies at most 2 segments before g. In every draw the first 3 segments form one chain, each the child of the one before, and so do the last 3.
All inputs are finite; a program needn't handle non-finite values. No bound on the sum of `loss_mask` on one device may be relied on, other than what follows from the above.
Results may differ from the reference program's by a relative error of at most 0.028.
Values may be sent and summed in bfloat16 or wider, within the bound.
A program may use at most 64 MiB of HBM per device.

```python
import math
import jax
import jax.numpy as jnp
from jax import lax

QUERY_HEAD_COUNT = 32
KEY_VALUE_HEADS = 8
HEAD_SIZE = 128
SEGMENT_LENGTH = 512
ANCESTOR_SPAN = 2
SEGMENT_TOTAL = 64
TOKEN_TOTAL = 32768


def draw_queries(key, part):
    key = jax.random.fold_in(key, 11)
    final_output = jnp.clip(jax.random.normal(key, (TOKEN_TOTAL, KEY_VALUE_HEADS, QUERY_HEAD_COUNT // KEY_VALUE_HEADS, HEAD_SIZE), jnp.float32), -5.0, 5.0)
    return final_output.reshape(TOKEN_TOTAL, QUERY_HEAD_COUNT * HEAD_SIZE).astype(jnp.bfloat16)


def draw_keys(key, part):
    key = jax.random.fold_in(key, 23)
    final_output = jnp.clip(jax.random.normal(key, (TOKEN_TOTAL, KEY_VALUE_HEADS, HEAD_SIZE), jnp.float32), -5.0, 5.0)
    return final_output.reshape(TOKEN_TOTAL, KEY_VALUE_HEADS * HEAD_SIZE).astype(jnp.bfloat16)


def draw_parents(key, part):
    key = jax.random.fold_in(key, 37)
    key_coins, key_picks = jax.random.split(key, 2)
    coins = jax.random.randint(key_coins, (SEGMENT_TOTAL,), 0, 2)
    picks = jax.random.randint(key_picks, (SEGMENT_TOTAL,), 0, 1 << 20)
    slot_ids = jnp.arange(SEGMENT_TOTAL, dtype=jnp.int32)
    end_start = SEGMENT_TOTAL - 1 - ANCESTOR_SPAN
    inside = (slot_ids > 0) & (slot_ids <= ANCESTOR_SPAN) | (slot_ids > end_start)
    forced = (slot_ids == 0) | (slot_ids == ANCESTOR_SPAN + 1) | (slot_ids == end_start)

    def walk(last_start, inputs):
        segment, coin, pick, within, pinned = inputs
        starts = (segment == 0) | pinned | (coin == 1) & jnp.logical_not(within) | (segment - last_start > ANCESTOR_SPAN)
        new_start = jnp.where(starts, segment, last_start)
        span_size = jnp.maximum(segment - new_start, 1)
        parent = jnp.where(starts, -1, jnp.where(within, segment - 1, new_start + pick % span_size))
        return (new_start, parent.astype(jnp.int32))
    last_start, parents = lax.scan(walk, jnp.int32(0), (slot_ids, coins, picks, inside, forced))
    return parents


def place_ends(result, own_key, low, largest):
    longest = result.shape.index(max(result.shape))
    spots = []
    for shift in (0, 1):
        where = [jax.random.randint(jax.random.fold_in(own_key, axis), (), 0, length) for axis, length in enumerate(result.shape)]
        where[longest] = (where[longest] + shift) % result.shape[longest]
        spots.append(tuple(where))
    return result.at[spots[0]].set(low).at[spots[1]].set(largest)


def steps_of(stream_key, shape, pieces, smallest, high):
    level, own = 1.0, jax.random.fold_in(stream_key, 6)
    for position, parts in pieces:
        draws = jnp.exp(jax.random.uniform(jax.random.fold_in(own, position), (parts,), jnp.float32, smallest / len(pieces), high / len(pieces)))
        level = level * jnp.repeat(draws, shape[position] // parts).reshape([-1 if axis == position else 1 for axis in range(len(shape))])
    return level


def centred(stream_key, dims, scale, bound, cuts=(), kind=jnp.bfloat16):
    gain = steps_of(stream_key, dims, cuts, -0.22, 0.18) if cuts else 1.0
    array = jax.random.normal(stream_key, dims, jnp.float32) * scale * gain
    return jnp.minimum(jnp.maximum(array, -bound), bound).astype(kind)


def setup_inputs(seed: int = 0) -> dict:
    splits = jax.random.split(jax.random.key(seed), 8)
    return {
        "queries": draw_queries(jax.random.fold_in(splits[7], 71), 0),
        "keys": draw_keys(jax.random.fold_in(splits[7], 71), 0),
        "values": centred(splits[2], (TOKEN_TOTAL, KEY_VALUE_HEADS * HEAD_SIZE), 1.0, 5.0, ((0, 512),)),
        "upstream": centred(splits[3], (TOKEN_TOTAL, QUERY_HEAD_COUNT * HEAD_SIZE), (4 * TOKEN_TOTAL), 786432.0, ((0, 64), (1, 8))),
        "loss_mask": place_ends((jax.random.randint(splits[4], (TOKEN_TOTAL,), 0, 4) < 3).astype(jnp.int32), jax.random.fold_in(splits[4], 1), 0, 1),
        "parents": draw_parents(jax.random.fold_in(splits[7], 71), 0),
        "token_count": jax.random.randint(splits[6], (1,), TOKEN_TOTAL // 4, TOKEN_TOTAL + 1).astype(jnp.int32),
    }


def ancestry_table(parents):
    count_segments = parents.shape[0]
    slot_ids = jnp.arange(count_segments, dtype=jnp.int32)
    current = parents
    ancestry = [jnp.zeros((count_segments,), jnp.bool_) for segment_gap in range(ANCESTOR_SPAN)]
    for walk_step in range(ANCESTOR_SPAN):
        for segment_gap in range(1, ANCESTOR_SPAN + 1):
            matched = (current >= 0) & (current == slot_ids - segment_gap)
            ancestry[segment_gap - 1] = ancestry[segment_gap - 1] | matched
        safe_index = jnp.maximum(current, 0).astype(jnp.int32)
        current = jnp.where(current >= 0, parents[safe_index], -1).astype(jnp.int32)
    return jnp.stack(ancestry, axis=1)

def reference(queries, keys, values, upstream, loss_mask, parents, token_count):
    query_head_group = QUERY_HEAD_COUNT // KEY_VALUE_HEADS
    score_scale = 1.0 / math.sqrt(HEAD_SIZE)
    exact_mode = lax.Precision.HIGHEST
    ancestry = ancestry_table(parents)
    query_block_rows = queries.reshape(SEGMENT_TOTAL, SEGMENT_LENGTH, KEY_VALUE_HEADS, query_head_group, HEAD_SIZE)
    key_block_rows = keys.reshape(SEGMENT_TOTAL, SEGMENT_LENGTH, KEY_VALUE_HEADS, HEAD_SIZE)
    value_block_rows = values.reshape(SEGMENT_TOTAL, SEGMENT_LENGTH, KEY_VALUE_HEADS, HEAD_SIZE)
    zero_padding = jnp.zeros((ANCESTOR_SPAN, SEGMENT_LENGTH, KEY_VALUE_HEADS, HEAD_SIZE), keys.dtype)
    padded_keys = jnp.concatenate([zero_padding, key_block_rows], axis=0)
    padded_values = jnp.concatenate([zero_padding, value_block_rows], axis=0)
    token_weight = loss_mask.reshape(SEGMENT_TOTAL, SEGMENT_LENGTH).astype(jnp.float32) / token_count[0].astype(jnp.float32)
    upstream_gradient_blocks = upstream.reshape(SEGMENT_TOTAL, SEGMENT_LENGTH, KEY_VALUE_HEADS, query_head_group, HEAD_SIZE)
    positions = jnp.arange(SEGMENT_LENGTH, dtype=jnp.int32)
    causal = positions[:, None] >= positions[None, :]

    def per_segment(segment):
        seg_queries = query_block_rows[segment].astype(jnp.float32)
        ancestor_key_rows = lax.dynamic_slice_in_dim(padded_keys, segment, ANCESTOR_SPAN + 1, 0)
        ancestor_key_rows = ancestor_key_rows.reshape((ANCESTOR_SPAN + 1) * SEGMENT_LENGTH, KEY_VALUE_HEADS, HEAD_SIZE).astype(jnp.float32)
        ancestor_value_rows = lax.dynamic_slice_in_dim(padded_values, segment, ANCESTOR_SPAN + 1, 0)
        ancestor_value_rows = ancestor_value_rows.reshape((ANCESTOR_SPAN + 1) * SEGMENT_LENGTH, KEY_VALUE_HEADS, HEAD_SIZE).astype(jnp.float32)
        visible = [jnp.broadcast_to(ancestry[segment, ANCESTOR_SPAN - 1 - block_index], (SEGMENT_LENGTH, SEGMENT_LENGTH)) for block_index in range(ANCESTOR_SPAN)]
        allowed = jnp.concatenate(visible + [causal], axis=1)
        scores = jnp.einsum('tkgd,skd->kgts', seg_queries, ancestor_key_rows, precision=exact_mode) * score_scale
        scores = jnp.where(allowed, scores, -jnp.inf)
        row_max = lax.optimization_barrier(jnp.max(scores, axis=-1))
        lse = row_max + jnp.log(lax.optimization_barrier(jnp.sum(jnp.exp(scores - row_max[..., None]), axis=-1)))
        probs = jnp.exp(scores - lse[..., None]).astype(jnp.bfloat16)
        probs_wide = lax.optimization_barrier(probs).astype(jnp.float32)
        attended = jnp.einsum('kgts,skd->tkgd', probs_wide, ancestor_value_rows, precision=exact_mode).astype(jnp.bfloat16)
        grad_out = (upstream_gradient_blocks[segment].astype(jnp.float32) * token_weight[segment][:, None, None, None]).astype(jnp.bfloat16)
        grad_wide = lax.optimization_barrier(grad_out).astype(jnp.float32)
        attended_wide = lax.optimization_barrier(attended).astype(jnp.float32)
        delta = lax.optimization_barrier(jnp.sum(grad_wide * attended_wide, axis=-1)).transpose(1, 2, 0)
        dprob = jnp.einsum('tkgd,skd->kgts', grad_wide, ancestor_value_rows, precision=exact_mode)
        dscore = (probs_wide * (dprob - delta[..., None])).astype(jnp.bfloat16)
        dscore = lax.optimization_barrier(dscore).astype(jnp.float32)
        query_gradient = (jnp.einsum('kgts,skd->tkgd', dscore, ancestor_key_rows, precision=exact_mode) * score_scale).astype(jnp.bfloat16)
        key_gradient = jnp.einsum('kgts,tkgd->skd', dscore, seg_queries, precision=exact_mode) * score_scale
        value_gradient = jnp.einsum('kgts,tkgd->skd', probs_wide, grad_wide, precision=exact_mode)
        return (attended, query_gradient, key_gradient.reshape(ANCESTOR_SPAN + 1, SEGMENT_LENGTH, KEY_VALUE_HEADS, HEAD_SIZE), value_gradient.reshape(ANCESTOR_SPAN + 1, SEGMENT_LENGTH, KEY_VALUE_HEADS, HEAD_SIZE))
    attended, query_gradient, key_terms, value_terms = lax.map(per_segment, jnp.arange(SEGMENT_TOTAL, dtype=jnp.int32))
    key_block_total = jnp.zeros((SEGMENT_TOTAL, SEGMENT_LENGTH, KEY_VALUE_HEADS, HEAD_SIZE), jnp.float32)
    value_block_total = jnp.zeros((SEGMENT_TOTAL, SEGMENT_LENGTH, KEY_VALUE_HEADS, HEAD_SIZE), jnp.float32)
    for segment_gap in range(ANCESTOR_SPAN + 1):
        zero_trailer = jnp.zeros((segment_gap, SEGMENT_LENGTH, KEY_VALUE_HEADS, HEAD_SIZE), jnp.float32)
        key_block_total = key_block_total + jnp.concatenate([key_terms[segment_gap:, ANCESTOR_SPAN - segment_gap], zero_trailer], axis=0)
        value_block_total = value_block_total + jnp.concatenate([value_terms[segment_gap:, ANCESTOR_SPAN - segment_gap], zero_trailer], axis=0)
    return (attended.reshape(TOKEN_TOTAL, QUERY_HEAD_COUNT * HEAD_SIZE), query_gradient.reshape(TOKEN_TOTAL, QUERY_HEAD_COUNT * HEAD_SIZE), key_block_total.astype(jnp.bfloat16).reshape(TOKEN_TOTAL, KEY_VALUE_HEADS * HEAD_SIZE), value_block_total.astype(jnp.bfloat16).reshape(TOKEN_TOTAL, KEY_VALUE_HEADS * HEAD_SIZE))
```

```python
import math

import jax
import jax.numpy as jnp
from jax import lax
from jax.experimental import pallas as pl
from jax.experimental.pallas import tpu as pltpu
from jax.sharding import PartitionSpec as P

F32 = jnp.float32
BF16 = jnp.bfloat16
TOKENS = 512
HEADS = 4
SIZE = 128
PIECE = 64
PEERS = 8
BLOCK = 256
CHUNKS = 4
CHUNK = TOKENS // CHUNKS
SCALE = 1.0 / math.sqrt(SIZE)
EXP_SCALE = math.log2(math.e) * SCALE
NEGATIVE = -1e30
MESH = pl.DeviceIdType.MESH
STEPS = [(1, 0), (1, 1), (1, 3), (1, 2), (0, 1), (0, 3), (0, 2)]


def dot(a, b, transposed=False):
    dims = (((1,), (1 if transposed else 0,)), ((), ()))
    return lax.dot_general(a, b, dims, preferred_element_type=F32)


def ancestor_seen(parents_ref, segment):
    first = parents_ref[segment]
    second = jnp.where(first >= 0, parents_ref[jnp.maximum(first, 0)], -1)
    seen = []
    for gap in (1, 2):
        wanted = segment - gap
        seen.append((wanted >= 0) & ((first == wanted) | (second == wanted)))
    return seen


def kernel(
    q_hbm, k_hbm, v_hbm, up_hbm, mask_ref, parents_ref, count_ref,
    att_hbm, dq_hbm, dk_hbm, dv_hbm,
    q_in, kv, up, stacked_q, stacked_g, kv_t, probs, scores, delta, dq_t, dscore,
    att, dq, ret_tx, ret_rx, own_grad, own_out,
    kv_sem, q_sem, gap_sem, ret_sem, send_sem, local_sem,
):
    segment = lax.axis_index("seq")
    group = lax.axis_index("head")
    odd = segment % 2
    sibling = segment + 1 - 2 * odd
    last = 64
    x, y = group // 4, group % 4

    my_rows = pl.ds(pl.multiple_of(group * PIECE, PIECE), PIECE)
    my_kv_cols = pl.ds(pl.multiple_of(group * SIZE, SIZE), SIZE)
    my_q_cols = pl.ds(pl.multiple_of(group * HEADS * SIZE, HEADS * SIZE), HEADS * SIZE)
    my_chunk = group // (CHUNK // PIECE)
    own_copies = [
        pltpu.make_async_copy(k_hbm.at[:, my_kv_cols], kv.at[0, 0, my_rows, :], local_sem.at[0]),
        pltpu.make_async_copy(v_hbm.at[:, my_kv_cols], kv.at[0, 1, my_rows, :], local_sem.at[1]),
        pltpu.make_async_copy(q_hbm.at[:, my_q_cols], q_in.at[my_rows, :], local_sem.at[2]),
        pltpu.make_async_copy(up_hbm, up, local_sem.at[3]),
    ]
    for copy in own_copies:
        copy.start()

    barrier = pltpu.get_barrier_semaphore()
    peers = []
    for x_step, y_step in STEPS:
        peer = (x + x_step) % 2 * 4 + (y + y_step) % 4
        peers.append(peer)
        pl.semaphore_signal(barrier, inc=1, device_id={"head": peer}, device_id_type=MESH)
    pl.semaphore_signal(barrier, inc=1, device_id={"seq": sibling}, device_id_type=MESH)
    has_next = segment < last - 2
    has_before = segment >= 2

    for other in ((segment + 2) % last, (segment + last - 2) % last):
        pl.semaphore_signal(barrier, inc=1, device_id={"seq": other}, device_id_type=MESH)
    pl.semaphore_wait(barrier, 10)

    sends = []

    def send(src, dst, recv, device):
        copy = pltpu.make_async_remote_copy(
            src_ref=src, dst_ref=dst, send_sem=send_sem.at[len(sends)], recv_sem=recv,
            device_id=device, device_id_type=MESH,
        )
        copy.start()
        sends.append(copy)

    for n, peer in enumerate(peers):
        cols = pl.ds(pl.multiple_of(peer * SIZE, SIZE), SIZE)
        send(k_hbm.at[:, cols], kv.at[0, 0, my_rows, :], kv_sem.at[0, group], {"head": peer})
        send(v_hbm.at[:, cols], kv.at[0, 1, my_rows, :], kv_sem.at[1, group], {"head": peer})
    for n, peer in enumerate(peers):
        cols = pl.ds(pl.multiple_of(peer * HEADS * SIZE, HEADS * SIZE), HEADS * SIZE)
        send(q_hbm.at[:, cols], q_in.at[my_rows, :], q_sem.at[group], {"head": peer})

    def wait_for(ref, sem):
        pltpu.make_async_copy(ref, ref, sem).wait()

    own_copies[0].wait()
    own_copies[1].wait()

    def to_next(c, start):
        rows = pl.ds(c * CHUNK, CHUNK)
        return pltpu.make_async_remote_copy(
            src_ref=kv.at[0, :, rows, :], dst_ref=kv.at[2, :, rows, :],
            send_sem=send_sem.at[32 + c], recv_sem=gap_sem.at[1, c],
            device_id={"seq": segment + 2}, device_id_type=MESH,
        )

    def to_sibling(c, source):
        rows = pl.ds(c * CHUNK, CHUNK)
        return pltpu.make_async_remote_copy(
            src_ref=kv.at[source, :, rows, :], dst_ref=kv.at[1, :, rows, :],
            send_sem=send_sem.at[36 + c], recv_sem=gap_sem.at[0, c],
            device_id={"seq": sibling}, device_id_type=MESH,
        )

    for c in range(CHUNKS):
        for r in range(c * CHUNK // PIECE, (c + 1) * CHUNK // PIECE):

            @pl.when(group != r)
            def _():
                wait_for(kv.at[0, 0, pl.ds(r * PIECE, PIECE), :], kv_sem.at[0, r])
                wait_for(kv.at[0, 1, pl.ds(r * PIECE, PIECE), :], kv_sem.at[1, r])

        @pl.when(has_next)
        def _():
            to_next(c, True).start()

        @pl.when(odd == 0)
        def _():
            to_sibling(c, 0).start()

    for c in range(CHUNKS):

        @pl.when(has_before)
        def _():
            wait_for(kv.at[2, :, pl.ds(c * CHUNK, CHUNK), :], gap_sem.at[1, c])

        @pl.when(has_before & (odd == 1))
        def _():
            to_sibling(c, 2).start()

    @pl.when(segment < 2)
    def _():
        kv[2] = jnp.zeros(kv.shape[1:], BF16)

    @pl.when(segment == 0)
    def _():
        kv[1] = jnp.zeros(kv.shape[1:], BF16)

    own_copies[2].wait()
    for r in range(PEERS):

        @pl.when(group != r)
        def _():
            wait_for(q_in.at[pl.ds(r * PIECE, PIECE), :], q_sem.at[r])

    for h in range(HEADS):
        stacked_q[h * TOKENS : (h + 1) * TOKENS, :] = q_in[:, h * SIZE : (h + 1) * SIZE]

    @pl.when(segment > 0)
    def _():
        for c in range(CHUNKS):
            wait_for(kv.at[1, :, pl.ds(c * CHUNK, CHUNK), :], gap_sem.at[0, c])

    for t in range(3):
        for i in range(2):
            kv_t[t, i] = kv[t, i].T
    own_copies[3].wait()

    seen = ancestor_seen(parents_ref, segment)
    weight = mask_ref[...].astype(F32) / count_ref[0].astype(F32)
    causal = lax.broadcasted_iota(jnp.int32, (BLOCK, BLOCK), 0) <= lax.broadcasted_iota(
        jnp.int32, (BLOCK, BLOCK), 1
    )
    for half in range(2):
        tok = slice(half * BLOCK, (half + 1) * BLOCK)
        tiles = [(2, 0), (2, BLOCK), (1, 0), (1, BLOCK)] + [(0, r) for r in range(0, (half + 1) * BLOCK, BLOCK)]
        for h in range(HEADS):
            rows = slice(h * TOKENS + half * BLOCK, h * TOKENS + (half + 1) * BLOCK)
            cols = slice(h * SIZE, (h + 1) * SIZE)
            slot = h % 2
            query = stacked_q[rows, :]
            tops = [None, None, None]
            for n, (t, r) in enumerate(tiles):
                s = dot(kv[t, 0, r : r + BLOCK, :], query, transposed=True)
                if t == 0 and r == half * BLOCK:
                    s = jnp.where(causal, s, NEGATIVE)
                scores[slot, n] = s
                top = jnp.max(s.reshape(BLOCK // 8, 8, BLOCK), axis=0)
                tops[t] = top if tops[t] is None else jnp.maximum(tops[t], top)
            top = tops[0]
            for gap in (1, 2):
                top = jnp.maximum(top, jnp.where(seen[gap - 1], tops[gap], NEGATIVE))
            top = jnp.max(top, axis=0, keepdims=True) * EXP_SCALE
            shifts = [top] + [jnp.where(seen[gap - 1], top, -NEGATIVE) for gap in (1, 2)]
            total, out = None, None
            for n, (t, r) in enumerate(tiles):
                e = jnp.exp2(scores[slot, n] * EXP_SCALE - shifts[t])
                part = jnp.sum(e.reshape(BLOCK // 8, 8, BLOCK), axis=0)
                total = part if total is None else total + part
                e = e.astype(BF16)
                probs[t, r : r + BLOCK, rows] = e
                o = dot(kv_t[t, 1, :, r : r + BLOCK], e)
                out = o if out is None else out + o
            inverse = 1.0 / jnp.sum(total, axis=0, keepdims=True)
            out = (out * inverse).T.astype(BF16)
            att[tok, cols] = out
            factor = jnp.broadcast_to(weight[0:1, tok] * inverse, (SIZE, BLOCK)).T
            g = (up[tok, cols].astype(F32) * factor).astype(BF16)
            stacked_g[rows, :] = g
            product = (g.astype(F32) * out.astype(F32)).T
            delta[0:1, rows] = jnp.sum(product, axis=0, keepdims=True)
    att_out = pltpu.make_async_copy(att, att_hbm, local_sem.at[4])
    att_out.start()

    def backward(t, first):
        def step(n):
            rows = slice(n * BLOCK, (n + 1) * BLOCK)
            d = dot(kv[t, 1], stacked_g[rows, :], transposed=True)
            d = (probs[t, :, rows].astype(F32) * (d - delta[0:1, rows])).astype(BF16)
            dscore[:, rows] = d
            part = dot(kv_t[t, 0], d)
            dq_t[:, rows] = part if first else dq_t[:, rows] + part

        for n in range(2 * HEADS):
            step(n)
        return dot(dscore[...], stacked_q[...]) * SCALE, dot(probs[t], stacked_g[...])

    dk, dv = backward(1 + odd, True)
    ret_tx[0, 0] = dk.astype(BF16)
    ret_tx[0, 1] = dv.astype(BF16)

    def part_copy(slot):
        return pltpu.make_async_remote_copy(
            src_ref=ret_tx.at[slot], dst_ref=ret_rx.at[0],
            send_sem=send_sem.at[40 + slot], recv_sem=ret_sem.at[0],
            device_id={"seq": sibling}, device_id_type=MESH,
        )

    def back_copy(slot):
        return pltpu.make_async_remote_copy(
            src_ref=ret_tx.at[slot], dst_ref=ret_rx.at[1],
            send_sem=send_sem.at[42 + slot], recv_sem=ret_sem.at[1],
            device_id={"seq": segment - 2}, device_id_type=MESH,
        )

    @pl.when(odd == 0)
    def _():
        part_copy(0).start()

    @pl.when(odd == 1)
    def _():
        wait_for(ret_rx.at[0], ret_sem.at[0])
        for i in range(2):
            ret_tx[0, i] = (ret_tx[0, i].astype(F32) + ret_rx[0, i].astype(F32)).astype(BF16)

    @pl.when((odd == 1) & has_before)
    def _():
        back_copy(0).start()

    dk, dv = backward(2 - odd, False)
    ret_tx[1, 0] = dk.astype(BF16)
    ret_tx[1, 1] = dv.astype(BF16)

    @pl.when(odd == 1)
    def _():
        part_copy(1).start()

    @pl.when((odd == 0) & has_before)
    def _():
        back_copy(1).start()

    for half in range(2):
        seen_rows = (half + 1) * BLOCK
        tok = slice(half * BLOCK, (half + 1) * BLOCK)
        for h in range(HEADS):
            rows = slice(h * TOKENS + half * BLOCK, h * TOKENS + (half + 1) * BLOCK)
            d = dot(kv[0, 1, 0:seen_rows, :], stacked_g[rows, :], transposed=True)
            d = (probs[0, 0:seen_rows, rows].astype(F32) * (d - delta[0:1, rows])).astype(BF16)
            dscore[0:seen_rows, rows] = d
            total = dq_t[:, rows] + dot(kv_t[0, 0, :, 0:seen_rows], d)
            dq[tok, h * SIZE : (h + 1) * SIZE] = (total * SCALE).T.astype(BF16)
    dq_out = pltpu.make_async_copy(dq, dq_hbm, local_sem.at[5])
    dq_out.start()
    own_grad[0, 0:BLOCK] = dot(dscore[0:BLOCK, :], stacked_q[...]) * SCALE
    own_grad[1, 0:BLOCK] = dot(probs[0, 0:BLOCK, :], stacked_g[...])
    dk, dv = None, None
    for h in range(HEADS):
        rows = slice(h * TOKENS + BLOCK, (h + 1) * TOKENS)
        a = dot(dscore[BLOCK:, rows], stacked_q[rows, :])
        b = dot(probs[0, BLOCK:, rows], stacked_g[rows, :])
        dk = a if dk is None else dk + a
        dv = b if dv is None else dv + b
    own_grad[0, BLOCK:] = dk * SCALE
    own_grad[1, BLOCK:] = dv

    @pl.when(odd == 0)
    def _():
        wait_for(ret_rx.at[0], ret_sem.at[0])
        for i in range(2):
            own_grad[i] = own_grad[i] + ret_rx[0, i].astype(F32)

    @pl.when(has_next)
    def _():
        wait_for(ret_rx.at[1], ret_sem.at[1])
        for i in range(2):
            own_grad[i] = own_grad[i] + ret_rx[1, i].astype(F32)

    for i in range(2):
        own_out[i] = own_grad[i].astype(BF16)
    outs = [
        pltpu.make_async_copy(own_out.at[0], dk_hbm, local_sem.at[6]),
        pltpu.make_async_copy(own_out.at[1], dv_hbm, local_sem.at[7]),
    ]
    for copy in outs:
        copy.start()

    for copy in sends:
        copy.wait_send()
    for c in range(CHUNKS):

        @pl.when(has_next)
        def _():
            to_next(c, False).wait_send()

        @pl.when((odd == 0) | has_before)
        def _():
            to_sibling(c, 0).wait_send()

    @pl.when(odd == 0)
    def _():
        part_copy(0).wait_send()

    @pl.when(odd == 1)
    def _():
        part_copy(1).wait_send()

    @pl.when((odd == 1) & has_before)
    def _():
        back_copy(0).wait_send()

    @pl.when((odd == 0) & has_before)
    def _():
        back_copy(1).wait_send()

    att_out.wait()
    dq_out.wait()
    for copy in outs:
        copy.wait()


def per_device(queries, keys, values, upstream, loss_mask, parents, token_count):
    hbm = pl.BlockSpec(memory_space=pl.ANY)
    smem = pl.BlockSpec(memory_space=pltpu.SMEM)
    wide = jax.ShapeDtypeStruct((TOKENS, HEADS * SIZE), BF16)
    narrow = jax.ShapeDtypeStruct((TOKENS, SIZE), BF16)
    rows = HEADS * TOKENS
    return pl.pallas_call(
        kernel,
        out_shape=(wide, wide, narrow, narrow),
        in_specs=[hbm, hbm, hbm, hbm, pl.BlockSpec(memory_space=pltpu.VMEM), smem, smem],
        out_specs=[hbm] * 4,
        scratch_shapes=[
            pltpu.VMEM((TOKENS, HEADS * SIZE), BF16),
            pltpu.VMEM((3, 2, TOKENS, SIZE), BF16),
            pltpu.VMEM((TOKENS, HEADS * SIZE), BF16),
            pltpu.VMEM((rows, SIZE), BF16),
            pltpu.VMEM((rows, SIZE), BF16),
            pltpu.VMEM((3, 2, SIZE, TOKENS), BF16),
            pltpu.VMEM((3, TOKENS, rows), BF16),
            pltpu.VMEM((2, 6, BLOCK, BLOCK), F32),
            pltpu.VMEM((8, rows), F32),
            pltpu.VMEM((SIZE, rows), F32),
            pltpu.VMEM((TOKENS, rows), BF16),
            pltpu.VMEM((TOKENS, HEADS * SIZE), BF16),
            pltpu.VMEM((TOKENS, HEADS * SIZE), BF16),
            pltpu.VMEM((2, 2, TOKENS, SIZE), BF16),
            pltpu.VMEM((2, 2, TOKENS, SIZE), BF16),
            pltpu.VMEM((2, TOKENS, SIZE), F32),
            pltpu.VMEM((2, TOKENS, SIZE), BF16),
            pltpu.SemaphoreType.DMA((2, PEERS)),
            pltpu.SemaphoreType.DMA((PEERS,)),
            pltpu.SemaphoreType.DMA((2, CHUNKS)),
            pltpu.SemaphoreType.DMA((2,)),
            pltpu.SemaphoreType.DMA((44,)),
            pltpu.SemaphoreType.DMA((8,)),
        ],
        compiler_params=pltpu.CompilerParams(
            collective_id=0, has_side_effects=True, vmem_limit_bytes=62 << 20
        ),
        cost_estimate=pl.CostEstimate(flops=5 * 10**9, bytes_accessed=3 * 10**6, transcendentals=3 * 10**6),
    )(queries, keys, values, upstream, loss_mask.reshape(1, TOKENS), parents, token_count)


def solution(mesh):
    in_specs = (
        P(("seq", "head"), None),
        P(("seq", "head"), None),
        P(("seq", "head"), None),
        P("seq", "head"),
        P("seq"),
        P(),
        P(),
    )
    out_specs = (P("seq", "head"), P("seq", "head"), P("seq", "head"), P("seq", "head"))
    return jax.shard_map(
        per_device, mesh=mesh, in_specs=in_specs, out_specs=out_specs, check_vma=False
    )
```

```python
import math

import jax
import jax.numpy as jnp
from jax import lax
from jax.experimental import pallas as pl
from jax.experimental.pallas import tpu as pltpu
from jax.sharding import PartitionSpec as P

F32 = jnp.float32
BF16 = jnp.bfloat16
TOKENS = 512
HEADS = 4
SIZE = 128
PIECE = 64
PEERS = 8
BLOCK = 256
CHUNKS = 4
CHUNK = TOKENS // CHUNKS
SCALE = 1.0 / math.sqrt(SIZE)
EXP_SCALE = math.log2(math.e) * SCALE
NEGATIVE = -1e30
MESH = pl.DeviceIdType.MESH
STEPS = [(1, 0), (1, 1), (1, 3), (1, 2), (0, 1), (0, 3), (0, 2)]


def dot(a, b, transposed=False):
    dims = (((1,), (1 if transposed else 0,)), ((), ()))
    return lax.dot_general(a, b, dims, preferred_element_type=F32)


def ancestor_seen(parents_ref, segment):
    first = parents_ref[segment]
    second = jnp.where(first >= 0, parents_ref[jnp.maximum(first, 0)], -1)
    seen = []
    for gap in (1, 2):
        wanted = segment - gap
        seen.append((wanted >= 0) & ((first == wanted) | (second == wanted)))
    return seen


def kernel(
    q_hbm, k_hbm, v_hbm, up_hbm, mask_hbm, parents_hbm, count_ref,
    att, dq, dk_out, dv_out,
    q_in, kv, up, stacked_q, stacked_g, kv_t, probs, scores, delta, dq_t, dscore,
    ret_tx, ret_rx, own_grad, mask_ref, parents_ref,
    kv_sem, q_sem, gap_sem, ret_sem, send_sem, edge_sem, local_sem,
):
    segment = lax.axis_index("seq")
    group = lax.axis_index("head")
    odd = segment % 2
    sibling = segment + 1 - 2 * odd
    last = 64
    x, y = group // 4, group % 4

    my_rows = pl.ds(pl.multiple_of(group * PIECE, PIECE), PIECE)
    my_kv_cols = pl.ds(pl.multiple_of(group * SIZE, SIZE), SIZE)
    my_q_cols = pl.ds(pl.multiple_of(group * HEADS * SIZE, HEADS * SIZE), HEADS * SIZE)
    my_chunk = group // (CHUNK // PIECE)
    chip = segment // 2
    edge_source = chip // 15 - chip // 16 - chip // 30
    edge_target = chip // 16 - chip // 17
    own_copies = [
        pltpu.make_async_copy(k_hbm.at[:, my_kv_cols], kv.at[0, 0, my_rows, :], local_sem.at[0]),
        pltpu.make_async_copy(v_hbm.at[:, my_kv_cols], kv.at[0, 1, my_rows, :], local_sem.at[1]),
        pltpu.make_async_copy(q_hbm.at[:, my_q_cols], q_in.at[my_rows, :], local_sem.at[2]),
        pltpu.make_async_copy(up_hbm, up, local_sem.at[3]),
        pltpu.make_async_copy(mask_hbm, mask_ref, local_sem.at[4]),
        pltpu.make_async_copy(parents_hbm, parents_ref, local_sem.at[5]),
    ]
    for copy in own_copies:
        copy.start()

    barrier = pltpu.get_barrier_semaphore()
    peers = []
    for x_step, y_step in STEPS:
        peer = (x + x_step) % 2 * 4 + (y + y_step) % 4
        peers.append(peer)
        pl.semaphore_signal(barrier, inc=1, device_id={"head": peer}, device_id_type=MESH)
    pl.semaphore_signal(barrier, inc=1, device_id={"seq": sibling}, device_id_type=MESH)
    has_next = segment < last - 2
    has_before = segment >= 2


    def signal(**device):
        pl.semaphore_signal(barrier, inc=1, device_id=device, device_id_type=MESH)

    @pl.when(has_next & (edge_source == 0))
    def _():
        signal(seq=segment + 2)

    @pl.when(has_before & (edge_target == 0))
    def _():
        signal(seq=segment - 2)

    @pl.when(edge_source == 1)
    def _():
        for peer in range(PEERS):
            signal(seq=segment + 2, head=peer)

    @pl.when(edge_target == 1)
    def _():
        for peer in range(PEERS):
            signal(seq=segment - 2, head=peer)

    near = (segment + last - 2) // last + (2 * last - 3 - segment) // last
    pl.semaphore_wait(barrier, 8 + near + 7 * (edge_source + edge_target))

    sends = []

    def edge_copy(peer, i):
        cols = pl.ds(peer * SIZE, SIZE)
        return pltpu.make_async_remote_copy(
            src_ref=(k_hbm, v_hbm)[i].at[:, cols], dst_ref=kv.at[2, i, my_rows, :],
            send_sem=edge_sem.at[peer, i], recv_sem=gap_sem.at[1, my_chunk],
            device_id={"seq": segment + 2, "head": peer}, device_id_type=MESH,
        )

    @pl.when(edge_source == 1)
    def _():
        for peer in range(PEERS):
            for i in range(2):
                edge_copy(peer, i).start()

    def send(src, dst, recv, device):
        copy = pltpu.make_async_remote_copy(
            src_ref=src, dst_ref=dst, send_sem=send_sem.at[len(sends)], recv_sem=recv,
            device_id=device, device_id_type=MESH,
        )
        copy.start()
        sends.append(copy)

    for n, peer in enumerate(peers):
        cols = pl.ds(pl.multiple_of(peer * SIZE, SIZE), SIZE)
        send(k_hbm.at[:, cols], kv.at[0, 0, my_rows, :], kv_sem.at[0, group], {"head": peer})
        send(v_hbm.at[:, cols], kv.at[0, 1, my_rows, :], kv_sem.at[1, group], {"head": peer})
    for n, peer in enumerate(peers):
        cols = pl.ds(pl.multiple_of(peer * HEADS * SIZE, HEADS * SIZE), HEADS * SIZE)
        send(q_hbm.at[:, cols], q_in.at[my_rows, :], q_sem.at[group], {"head": peer})

    def wait_for(ref, sem):
        pltpu.make_async_copy(ref, ref, sem).wait()

    own_copies[0].wait()
    own_copies[1].wait()

    order = [(n + x * (CHUNKS // 2)) % CHUNKS for n in range(CHUNKS)]

    def chunk_rows(c):
        return pl.ds(pl.multiple_of(c * CHUNK, CHUNK), CHUNK)

    def to_next(c):
        return pltpu.make_async_remote_copy(
            src_ref=kv.at[0, :, chunk_rows(c), :], dst_ref=kv.at[2, :, chunk_rows(c), :],
            send_sem=send_sem.at[32 + c], recv_sem=gap_sem.at[1, c],
            device_id={"seq": segment + 2}, device_id_type=MESH,
        )

    def to_sibling(c, source):
        return pltpu.make_async_remote_copy(
            src_ref=kv.at[source, :, chunk_rows(c), :], dst_ref=kv.at[1, :, chunk_rows(c), :],
            send_sem=send_sem.at[36 + c], recv_sem=gap_sem.at[0, c],
            device_id={"seq": sibling}, device_id_type=MESH,
        )

    for c in order:
        for n in range(CHUNK // PIECE):
            r = c * (CHUNK // PIECE) + n
            rows = pl.ds(pl.multiple_of(r * PIECE, PIECE), PIECE)

            @pl.when(group != r)
            def _():
                wait_for(kv.at[0, 0, rows, :], kv_sem.at[0, r])
                wait_for(kv.at[0, 1, rows, :], kv_sem.at[1, r])

        @pl.when(has_next & (edge_source == 0))
        def _():
            to_next(c).start()

        @pl.when(odd == 0)
        def _():
            to_sibling(c, 0).start()

    for c in order:

        @pl.when(has_before)
        def _():
            wait_for(kv.at[2, :, chunk_rows(c), :], gap_sem.at[1, c])

        @pl.when(has_before & (odd == 1))
        def _():
            to_sibling(c, 2).start()

    @pl.when(segment < 2)
    def _():
        kv[2] = jnp.zeros(kv.shape[1:], BF16)

    @pl.when(segment == 0)
    def _():
        kv[1] = jnp.zeros(kv.shape[1:], BF16)

    own_copies[2].wait()
    for r in range(PEERS):

        @pl.when(group != r)
        def _():
            wait_for(q_in.at[pl.ds(r * PIECE, PIECE), :], q_sem.at[r])

    for h in range(HEADS):
        stacked_q[h * TOKENS : (h + 1) * TOKENS, :] = q_in[:, h * SIZE : (h + 1) * SIZE]

    @pl.when(segment > 0)
    def _():
        for c in range(CHUNKS):
            wait_for(kv.at[1, :, pl.ds(c * CHUNK, CHUNK), :], gap_sem.at[0, c])

    for t in range(3):
        for i in range(2):
            kv_t[t, i] = kv[t, i].T
    for copy in own_copies[3:]:
        copy.wait()

    seen = ancestor_seen(parents_ref, segment)
    weight = mask_ref[...].astype(F32) / count_ref[0].astype(F32)
    causal = lax.broadcasted_iota(jnp.int32, (BLOCK, BLOCK), 0) <= lax.broadcasted_iota(
        jnp.int32, (BLOCK, BLOCK), 1
    )
    for half in range(2):
        tok = slice(half * BLOCK, (half + 1) * BLOCK)
        tiles = [(2, 0), (2, BLOCK), (1, 0), (1, BLOCK)] + [(0, r) for r in range(0, (half + 1) * BLOCK, BLOCK)]
        for h in range(HEADS):
            rows = slice(h * TOKENS + half * BLOCK, h * TOKENS + (half + 1) * BLOCK)
            cols = slice(h * SIZE, (h + 1) * SIZE)
            slot = h % 2
            query = stacked_q[rows, :]
            tops = [None, None, None]
            for n, (t, r) in enumerate(tiles):
                s = dot(kv[t, 0, r : r + BLOCK, :], query, transposed=True)
                if t == 0 and r == half * BLOCK:
                    s = jnp.where(causal, s, NEGATIVE)
                scores[slot, n] = s
                top = jnp.max(s.reshape(BLOCK // 8, 8, BLOCK), axis=0)
                tops[t] = top if tops[t] is None else jnp.maximum(tops[t], top)
            top = tops[0]
            for gap in (1, 2):
                top = jnp.maximum(top, jnp.where(seen[gap - 1], tops[gap], NEGATIVE))
            top = jnp.max(top, axis=0, keepdims=True) * EXP_SCALE
            shifts = [top] + [jnp.where(seen[gap - 1], top, -NEGATIVE) for gap in (1, 2)]
            total, out = None, None
            for n, (t, r) in enumerate(tiles):
                e = jnp.exp2(scores[slot, n] * EXP_SCALE - shifts[t])
                part = jnp.sum(e.reshape(BLOCK // 8, 8, BLOCK), axis=0)
                total = part if total is None else total + part
                e = e.astype(BF16)
                probs[t, r : r + BLOCK, rows] = e
                o = dot(kv_t[t, 1, :, r : r + BLOCK], e)
                out = o if out is None else out + o
            inverse = 1.0 / jnp.sum(total, axis=0, keepdims=True)
            out = (out * inverse).T.astype(BF16)
            att[tok, cols] = out
            factor = jnp.broadcast_to(weight[0:1, tok] * inverse, (SIZE, BLOCK)).T
            g = (up[tok, cols].astype(F32) * factor).astype(BF16)
            stacked_g[rows, :] = g
            product = (g.astype(F32) * out.astype(F32)).T
            delta[0:1, rows] = jnp.sum(product, axis=0, keepdims=True)

    def backward(t, half, first):
        keys = slice(half * BLOCK, (half + 1) * BLOCK)
        for n in range(2 * HEADS):
            rows = slice(n * BLOCK, (n + 1) * BLOCK)
            d = dot(kv[t, 1, keys, :], stacked_g[rows, :], transposed=True)
            d = (probs[t, keys, rows].astype(F32) * (d - delta[0:1, rows])).astype(BF16)
            dscore[keys, rows] = d
            part = dot(kv_t[t, 0, :, keys], d)
            dq_t[:, rows] = part if first else dq_t[:, rows] + part
        ret_tx[t - 1, half, 0] = (dot(dscore[keys, :], stacked_q[...]) * SCALE).astype(BF16)
        ret_tx[t - 1, half, 1] = dot(probs[t, keys, :], stacked_g[...]).astype(BF16)

    def part_copy(half):
        return pltpu.make_async_remote_copy(
            src_ref=ret_tx.at[0, half], dst_ref=ret_rx.at[0, half],
            send_sem=send_sem.at[40 + half], recv_sem=ret_sem.at[0, half],
            device_id={"seq": sibling}, device_id_type=MESH,
        )

    def back_copy(half):
        return pltpu.make_async_remote_copy(
            src_ref=ret_tx.at[1, half], dst_ref=ret_rx.at[1, half],
            send_sem=send_sem.at[42 + half], recv_sem=ret_sem.at[1, half],
            device_id={"seq": segment - 2}, device_id_type=MESH,
        )

    for half in range(2):
        backward(2, half, half == 0)

        @pl.when((odd == 0) & has_before)
        def _():
            back_copy(half).start()

    for half in range(2):
        backward(1, half, False)
        part_copy(half).start()

    def join(half):
        @pl.when(odd == 1)
        def _():
            wait_for(ret_rx.at[0, half], ret_sem.at[0, half])
            ret_tx[1, half] = (ret_tx[1, half].astype(F32) + ret_rx[0, half].astype(F32)).astype(BF16)

        @pl.when((odd == 1) & has_before)
        def _():
            back_copy(half).start()

    join(0)

    for half in range(2):
        seen_rows = (half + 1) * BLOCK
        tok = slice(half * BLOCK, (half + 1) * BLOCK)
        for h in range(HEADS):
            rows = slice(h * TOKENS + half * BLOCK, h * TOKENS + (half + 1) * BLOCK)
            d = dot(kv[0, 1, 0:seen_rows, :], stacked_g[rows, :], transposed=True)
            d = (probs[0, 0:seen_rows, rows].astype(F32) * (d - delta[0:1, rows])).astype(BF16)
            dscore[0:seen_rows, rows] = d
            total = dq_t[:, rows] + dot(kv_t[0, 0, :, 0:seen_rows], d)
            dq[tok, h * SIZE : (h + 1) * SIZE] = (total * SCALE).T.astype(BF16)
        if half == 0:
            join(1)
    own_grad[0, 0:BLOCK] = dot(dscore[0:BLOCK, :], stacked_q[...]) * SCALE
    own_grad[1, 0:BLOCK] = dot(probs[0, 0:BLOCK, :], stacked_g[...])
    dk, dv = None, None
    for h in range(HEADS):
        rows = slice(h * TOKENS + BLOCK, (h + 1) * TOKENS)
        a = dot(dscore[BLOCK:, rows], stacked_q[rows, :])
        b = dot(probs[0, BLOCK:, rows], stacked_g[rows, :])
        dk = a if dk is None else dk + a
        dv = b if dv is None else dv + b
    own_grad[0, BLOCK:] = dk * SCALE
    own_grad[1, BLOCK:] = dv

    @pl.when(odd == 0)
    def _():
        for half in range(2):
            wait_for(ret_rx.at[0, half], ret_sem.at[0, half])
            for i in range(2):
                rows = slice(half * BLOCK, (half + 1) * BLOCK)
                own_grad[i, rows] = own_grad[i, rows] + ret_rx[0, half, i].astype(F32)

    @pl.when(has_next)
    def _():
        for half in range(2):
            wait_for(ret_rx.at[1, half], ret_sem.at[1, half])
            for i in range(2):
                rows = slice(half * BLOCK, (half + 1) * BLOCK)
                own_grad[i, rows] = own_grad[i, rows] + ret_rx[1, half, i].astype(F32)

    dk_out[...] = own_grad[0].astype(BF16)
    dv_out[...] = own_grad[1].astype(BF16)

    for copy in sends:
        copy.wait_send()

    @pl.when(edge_source == 1)
    def _():
        for peer in range(PEERS):
            for i in range(2):
                edge_copy(peer, i).wait_send()

    for c in range(CHUNKS):

        @pl.when(has_next & (edge_source == 0))
        def _():
            to_next(c).wait_send()

        @pl.when((odd == 0) | has_before)
        def _():
            to_sibling(c, 0).wait_send()

    for half in range(2):
        part_copy(half).wait_send()

        @pl.when(has_before)
        def _():
            back_copy(half).wait_send()


def deliver(*refs):
    copies = [pltpu.make_async_copy(refs[n], refs[n + 4], refs[8].at[n]) for n in range(4)]
    for copy in copies:
        copy.start()
    for copy in copies:
        copy.wait()


def per_device(queries, keys, values, upstream, loss_mask, parents, token_count):
    any_space = pl.BlockSpec(memory_space=pl.ANY)
    hbm = pl.BlockSpec(memory_space=pltpu.HBM)
    vmem = pl.BlockSpec(memory_space=pltpu.VMEM)
    smem = pl.BlockSpec(memory_space=pltpu.SMEM)
    shapes = [(TOKENS, HEADS * SIZE)] * 2 + [(TOKENS, SIZE)] * 2
    rows = HEADS * TOKENS
    operands = [
        pltpu.with_memory_space_constraint(a, pltpu.HBM)
        for a in (queries, keys, values, upstream, loss_mask.reshape(1, TOKENS), parents)
    ]
    parts = pl.pallas_call(
        kernel,
        out_shape=[pltpu.VMEM(shape, BF16) for shape in shapes],
        in_specs=[hbm] * 4 + [any_space] * 2 + [smem],
        out_specs=[vmem] * 4,
        scratch_shapes=[
            pltpu.VMEM((TOKENS, HEADS * SIZE), BF16),
            pltpu.VMEM((3, 2, TOKENS, SIZE), BF16),
            pltpu.VMEM((TOKENS, HEADS * SIZE), BF16),
            pltpu.VMEM((rows, SIZE), BF16),
            pltpu.VMEM((rows, SIZE), BF16),
            pltpu.VMEM((3, 2, SIZE, TOKENS), BF16),
            pltpu.VMEM((3, TOKENS, rows), BF16),
            pltpu.VMEM((2, 6, BLOCK, BLOCK), F32),
            pltpu.VMEM((8, rows), F32),
            pltpu.VMEM((SIZE, rows), F32),
            pltpu.VMEM((TOKENS, rows), BF16),
            pltpu.VMEM((2, 2, 2, BLOCK, SIZE), BF16),
            pltpu.VMEM((2, 2, 2, BLOCK, SIZE), BF16),
            pltpu.VMEM((2, TOKENS, SIZE), F32),
            pltpu.VMEM((1, TOKENS), jnp.int32),
            pltpu.SMEM((64,), jnp.int32),
            pltpu.SemaphoreType.DMA((2, PEERS)),
            pltpu.SemaphoreType.DMA((PEERS,)),
            pltpu.SemaphoreType.DMA((2, CHUNKS)),
            pltpu.SemaphoreType.DMA((2, 2)),
            pltpu.SemaphoreType.DMA((44,)),
            pltpu.SemaphoreType.DMA((PEERS, 2)),
            pltpu.SemaphoreType.DMA((6,)),
        ],
        compiler_params=pltpu.CompilerParams(
            collective_id=0, has_side_effects=True, vmem_limit_bytes=32 << 20
        ),
        cost_estimate=pl.CostEstimate(flops=5 * 10**9, bytes_accessed=3 * 10**6, transcendentals=3 * 10**6),
    )(*operands, token_count)
    return pl.pallas_call(
        deliver,
        out_shape=[jax.ShapeDtypeStruct(shape, BF16) for shape in shapes],
        in_specs=[vmem] * 4,
        out_specs=[hbm] * 4,
        scratch_shapes=[pltpu.SemaphoreType.DMA((4,))],
        compiler_params=pltpu.CompilerParams(vmem_limit_bytes=16 << 20),
    )(*parts)


def solution(mesh):
    in_specs = (
        P(("seq", "head"), None),
        P(("seq", "head"), None),
        P(("seq", "head"), None),
        P("seq", "head"),
        P("seq"),
        P(),
        P(),
    )
    out_specs = (P("seq", "head"), P("seq", "head"), P("seq", "head"), P("seq", "head"))
    return jax.shard_map(
        per_device, mesh=mesh, in_specs=in_specs, out_specs=out_specs, check_vma=False
    )
```

```python
import math

import jax
import jax.numpy as jnp
from jax import lax
from jax.experimental import pallas as pl
from jax.experimental.pallas import tpu as pltpu
from jax.sharding import PartitionSpec as P

F32 = jnp.float32
BF16 = jnp.bfloat16
TOKENS = 512
HEADS = 4
SIZE = 128
PIECE = 64
PEERS = 8
BLOCK = 256
CHUNKS = 4
CHUNK = TOKENS // CHUNKS
SCALE = 1.0 / math.sqrt(SIZE)
EXP_SCALE = math.log2(math.e) * SCALE
NEGATIVE = -1e30
MESH = pl.DeviceIdType.MESH
STEPS = [(1, 0), (1, 1), (1, 3), (1, 2), (0, 1), (0, 3), (0, 2)]


def dot(a, b, left=1, right=0):
    dims = (((left,), (right,)), ((), ()))
    return lax.dot_general(a, b, dims, preferred_element_type=F32)


def ancestor_seen(parents_ref, segment):
    first = parents_ref[segment]
    second = jnp.where(first >= 0, parents_ref[jnp.maximum(first, 0)], -1)
    seen = []
    for gap in (1, 2):
        wanted = segment - gap
        seen.append((wanted >= 0) & ((first == wanted) | (second == wanted)))
    return seen


def kernel(
    q_hbm, k_hbm, v_hbm, up_hbm, mask_hbm, parents_hbm, count_ref,
    att, dq, dk_out, dv_out,
    q_in, kv, up, stacked_q, stacked_g, v_t, probs, scores, delta, dscore,
    ret_tx, ret_rx, own_grad, mask_ref, parents_ref,
    kv_sem, q_sem, gap_sem, ret_sem, send_sem, edge_sem, local_sem,
):
    segment = lax.axis_index("seq")
    group = lax.axis_index("head")
    odd = segment % 2
    sibling = segment + 1 - 2 * odd
    last = 64
    x, y = group // 4, group % 4

    my_rows = pl.ds(pl.multiple_of(group * PIECE, PIECE), PIECE)
    my_kv_cols = pl.ds(pl.multiple_of(group * SIZE, SIZE), SIZE)
    my_q_cols = pl.ds(pl.multiple_of(group * HEADS * SIZE, HEADS * SIZE), HEADS * SIZE)
    my_chunk = group // (CHUNK // PIECE)
    chip = segment // 2
    edge_source = chip // 15 - chip // 16 - chip // 30
    edge_target = chip // 16 - chip // 17
    own_copies = [
        pltpu.make_async_copy(k_hbm.at[:, my_kv_cols], kv.at[0, my_rows, :], local_sem.at[0]),
        pltpu.make_async_copy(v_hbm.at[:, my_kv_cols], kv.at[1, my_rows, :], local_sem.at[1]),
        pltpu.make_async_copy(q_hbm.at[:, my_q_cols], q_in.at[my_rows, :], local_sem.at[2]),
        pltpu.make_async_copy(up_hbm, up, local_sem.at[3]),
        pltpu.make_async_copy(mask_hbm, mask_ref, local_sem.at[4]),
        pltpu.make_async_copy(parents_hbm, parents_ref, local_sem.at[5]),
    ]
    for copy in own_copies:
        copy.start()

    barrier = pltpu.get_barrier_semaphore()
    peers = []
    for x_step, y_step in STEPS:
        peer = (x + x_step) % 2 * 4 + (y + y_step) % 4
        peers.append(peer)
        pl.semaphore_signal(barrier, inc=1, device_id={"head": peer}, device_id_type=MESH)
    pl.semaphore_signal(barrier, inc=1, device_id={"seq": sibling}, device_id_type=MESH)
    has_next = segment < last - 2
    has_before = segment >= 2


    def signal(**device):
        pl.semaphore_signal(barrier, inc=1, device_id=device, device_id_type=MESH)

    @pl.when(has_before & (edge_target == 0))
    def _():
        signal(seq=segment - 2)

    @pl.when(edge_target == 1)
    def _():
        for peer in range(PEERS):
            signal(seq=segment - 2, head=peer)

    pl.semaphore_wait(barrier, 8 + (2 * last - 3 - segment) // last + 7 * edge_source)

    sends = []

    def edge_copy(peer, i):
        cols = pl.ds(peer * SIZE, SIZE)
        return pltpu.make_async_remote_copy(
            src_ref=(k_hbm, v_hbm)[i].at[:, cols], dst_ref=kv.at[i, pl.ds(pl.multiple_of(2 * TOKENS + group * PIECE, PIECE), PIECE), :],
            send_sem=edge_sem.at[peer, i], recv_sem=gap_sem.at[1, my_chunk],
            device_id={"seq": segment + 2, "head": peer}, device_id_type=MESH,
        )

    @pl.when(edge_source == 1)
    def _():
        for peer in range(PEERS):
            for i in range(2):
                edge_copy(peer, i).start()

    def send(src, dst, recv, device):
        copy = pltpu.make_async_remote_copy(
            src_ref=src, dst_ref=dst, send_sem=send_sem.at[len(sends)], recv_sem=recv,
            device_id=device, device_id_type=MESH,
        )
        copy.start()
        sends.append(copy)

    for n, peer in enumerate(peers):
        cols = pl.ds(pl.multiple_of(peer * SIZE, SIZE), SIZE)
        send(k_hbm.at[:, cols], kv.at[0, my_rows, :], kv_sem.at[0, group], {"head": peer})
        send(v_hbm.at[:, cols], kv.at[1, my_rows, :], kv_sem.at[1, group], {"head": peer})
    for n, peer in enumerate(peers):
        cols = pl.ds(pl.multiple_of(peer * HEADS * SIZE, HEADS * SIZE), HEADS * SIZE)
        send(q_hbm.at[:, cols], q_in.at[my_rows, :], q_sem.at[group], {"head": peer})

    def wait_for(ref, sem):
        pltpu.make_async_copy(ref, ref, sem).wait()

    own_copies[0].wait()
    own_copies[1].wait()

    order = [(n + x * (CHUNKS // 2)) % CHUNKS for n in range(CHUNKS)]

    def part_of(tile, c):
        return kv.at[:, pl.ds(pl.multiple_of(tile * TOKENS + c * CHUNK, CHUNK), CHUNK), :]

    def to_next(c):
        return pltpu.make_async_remote_copy(
            src_ref=part_of(0, c), dst_ref=part_of(2, c),
            send_sem=send_sem.at[32 + c], recv_sem=gap_sem.at[1, c],
            device_id={"seq": segment + 2}, device_id_type=MESH,
        )

    def to_sibling(c, source):
        return pltpu.make_async_remote_copy(
            src_ref=part_of(source, c), dst_ref=part_of(1, c),
            send_sem=send_sem.at[36 + c], recv_sem=gap_sem.at[0, c],
            device_id={"seq": sibling}, device_id_type=MESH,
        )

    for c in order:
        for n in range(CHUNK // PIECE):
            r = c * (CHUNK // PIECE) + n
            rows = pl.ds(pl.multiple_of(r * PIECE, PIECE), PIECE)

            @pl.when(group != r)
            def _():
                wait_for(kv.at[0, rows, :], kv_sem.at[0, r])
                wait_for(kv.at[1, rows, :], kv_sem.at[1, r])

        @pl.when(has_next & (edge_source == 0))
        def _():
            to_next(c).start()

        @pl.when(odd == 0)
        def _():
            to_sibling(c, 0).start()

    for c in order:

        @pl.when(has_before)
        def _():
            wait_for(part_of(2, c), gap_sem.at[1, c])

        @pl.when(has_before & (odd == 1))
        def _():
            to_sibling(c, 2).start()

    @pl.when(segment < 2)
    def _():
        kv[:, 2 * TOKENS :, :] = jnp.zeros((2, TOKENS, SIZE), BF16)

    @pl.when(segment == 0)
    def _():
        kv[:, TOKENS : 2 * TOKENS, :] = jnp.zeros((2, TOKENS, SIZE), BF16)

    own_copies[2].wait()
    for r in range(PEERS):

        @pl.when(group != r)
        def _():
            wait_for(q_in.at[pl.ds(r * PIECE, PIECE), :], q_sem.at[r])

    for h in range(HEADS):
        stacked_q[h * TOKENS : (h + 1) * TOKENS, :] = q_in[:, h * SIZE : (h + 1) * SIZE]

    @pl.when(segment > 0)
    def _():
        for c in range(CHUNKS):
            wait_for(part_of(1, c), gap_sem.at[0, c])

    for copy in own_copies[3:]:
        copy.wait()

    v_t[...] = kv[1].T

    seen = ancestor_seen(parents_ref, segment)
    weight = mask_ref[...].astype(F32) / count_ref[0].astype(F32)
    causal = lax.broadcasted_iota(jnp.int32, (BLOCK, BLOCK), 0) <= lax.broadcasted_iota(
        jnp.int32, (BLOCK, BLOCK), 1
    )

    def down(row):
        return jnp.broadcast_to(row, (SIZE, BLOCK)).T

    for half in range(2):
        tok = slice(half * BLOCK, (half + 1) * BLOCK)
        own_keys = (half + 1) * BLOCK
        blocks = list(range(TOKENS, 3 * TOKENS, BLOCK)) + list(range(0, own_keys, BLOCK))
        for h in range(HEADS):
            rows = slice(h * TOKENS + half * BLOCK, h * TOKENS + (half + 1) * BLOCK)
            cols = slice(h * SIZE, (h + 1) * SIZE)
            slot = h % 2
            query = stacked_q[rows, :]
            tops = [None, None, None]
            for n, r in enumerate(blocks):
                s = dot(kv[0, r : r + BLOCK, :], query, right=1)
                if r == half * BLOCK:
                    s = jnp.where(causal, s, NEGATIVE)
                scores[slot, n] = s
                t = r // TOKENS
                top = jnp.max(s.reshape(BLOCK // 8, 8, BLOCK), axis=0)
                tops[t] = top if tops[t] is None else jnp.maximum(tops[t], top)
            top = tops[0]
            for gap in (1, 2):
                top = jnp.maximum(top, jnp.where(seen[gap - 1], tops[gap], NEGATIVE))
            top = jnp.max(top, axis=0, keepdims=True) * EXP_SCALE
            shifts = [top] + [jnp.where(seen[gap - 1], top, -NEGATIVE) for gap in (1, 2)]
            total, out = None, None
            for n, r in enumerate(blocks):
                e = jnp.exp2(scores[slot, n] * EXP_SCALE - shifts[r // TOKENS])
                part = jnp.sum(e.reshape(BLOCK // 8, 8, BLOCK), axis=0)
                total = part if total is None else total + part
                e = e.astype(BF16)
                probs[r : r + BLOCK, rows] = e
                part = dot(v_t[:, r : r + BLOCK], e)
                out = part if out is None else out + part
            inverse = 1.0 / jnp.sum(total, axis=0, keepdims=True)
            out = (out * inverse).T.astype(BF16)
            att[tok, cols] = out
            g = (up[tok, cols].astype(F32) * down(weight[0:1, tok] * inverse)).astype(BF16)
            stacked_g[rows, :] = g
            product = (g.astype(F32) * out.astype(F32)).T
            delta[0:1, rows] = jnp.sum(product, axis=0, keepdims=True)

    def score_gradient(start, stop, rows):
        d = dot(kv[1, start:stop, :], stacked_g[rows, :], right=1)
        d = probs[start:stop, rows].astype(F32) * (d - delta[0:1, rows])
        dscore[start:stop, rows] = d.astype(BF16)

    def ancestor_scores(t):
        for n in range(2 * HEADS):
            score_gradient(t * TOKENS, (t + 1) * TOKENS, slice(n * BLOCK, (n + 1) * BLOCK))

    def ancestor_terms(t, half):
        keys = slice(t * TOKENS + half * BLOCK, t * TOKENS + (half + 1) * BLOCK)
        ret_tx[t - 1, half, 0] = (dot(dscore[keys, :], stacked_q[...]) * SCALE).astype(BF16)
        ret_tx[t - 1, half, 1] = dot(probs[keys, :], stacked_g[...]).astype(BF16)

    def part_copy(half):
        return pltpu.make_async_remote_copy(
            src_ref=ret_tx.at[0, half], dst_ref=ret_rx.at[0, half],
            send_sem=send_sem.at[40 + half], recv_sem=ret_sem.at[0, half],
            device_id={"seq": sibling}, device_id_type=MESH,
        )

    def back_copy(half):
        return pltpu.make_async_remote_copy(
            src_ref=ret_tx.at[1, half], dst_ref=ret_rx.at[1, half],
            send_sem=send_sem.at[42 + half], recv_sem=ret_sem.at[1, half],
            device_id={"seq": segment - 2}, device_id_type=MESH,
        )

    ancestor_scores(2)
    for half in range(2):
        ancestor_terms(2, half)

        @pl.when((odd == 0) & has_before)
        def _():
            back_copy(half).start()

    ancestor_scores(1)
    for half in range(2):
        ancestor_terms(1, half)
        part_copy(half).start()

    def join(half):
        @pl.when(odd == 1)
        def _():
            wait_for(ret_rx.at[0, half], ret_sem.at[0, half])
            ret_tx[1, half] = (ret_tx[1, half].astype(F32) + ret_rx[0, half].astype(F32)).astype(BF16)

        @pl.when((odd == 1) & has_before)
        def _():
            back_copy(half).start()

    for half in range(2):
        for h in range(HEADS):
            rows = slice(h * TOKENS + half * BLOCK, h * TOKENS + (half + 1) * BLOCK)
            score_gradient(0, (half + 1) * BLOCK, rows)
    own_grad[0, 0:BLOCK] = dot(dscore[0:BLOCK, :], stacked_q[...]) * SCALE
    own_grad[1, 0:BLOCK] = dot(probs[0:BLOCK, :], stacked_g[...])
    join(0)
    dk, dv = None, None
    for h in range(HEADS):
        rows = slice(h * TOKENS + BLOCK, (h + 1) * TOKENS)
        a = dot(dscore[BLOCK:TOKENS, rows], stacked_q[rows, :])
        b = dot(probs[BLOCK:TOKENS, rows], stacked_g[rows, :])
        dk = a if dk is None else dk + a
        dv = b if dv is None else dv + b
    own_grad[0, BLOCK:] = dk * SCALE
    own_grad[1, BLOCK:] = dv
    join(1)
    for half in range(2):
        own_keys = (half + 1) * BLOCK
        for h in range(HEADS):
            rows = slice(h * TOKENS + half * BLOCK, h * TOKENS + (half + 1) * BLOCK)
            total = dot(dscore[TOKENS:, rows], kv[0, TOKENS:, :], left=0) + dot(
                dscore[0:own_keys, rows], kv[0, 0:own_keys, :], left=0
            )
            tok = slice(half * BLOCK, (half + 1) * BLOCK)
            dq[tok, h * SIZE : (h + 1) * SIZE] = (total * SCALE).astype(BF16)

    @pl.when(odd == 0)
    def _():
        for half in range(2):
            wait_for(ret_rx.at[0, half], ret_sem.at[0, half])
            for i in range(2):
                rows = slice(half * BLOCK, (half + 1) * BLOCK)
                own_grad[i, rows] = own_grad[i, rows] + ret_rx[0, half, i].astype(F32)

    @pl.when(has_next)
    def _():
        for half in range(2):
            wait_for(ret_rx.at[1, half], ret_sem.at[1, half])
            for i in range(2):
                rows = slice(half * BLOCK, (half + 1) * BLOCK)
                own_grad[i, rows] = own_grad[i, rows] + ret_rx[1, half, i].astype(F32)

    dk_out[...] = own_grad[0].astype(BF16)
    dv_out[...] = own_grad[1].astype(BF16)

    for copy in sends:
        copy.wait_send()

    @pl.when(edge_source == 1)
    def _():
        for peer in range(PEERS):
            for i in range(2):
                edge_copy(peer, i).wait_send()

    for c in range(CHUNKS):

        @pl.when(has_next & (edge_source == 0))
        def _():
            to_next(c).wait_send()

        @pl.when((odd == 0) | has_before)
        def _():
            to_sibling(c, 0).wait_send()

    for half in range(2):
        part_copy(half).wait_send()

        @pl.when(has_before)
        def _():
            back_copy(half).wait_send()


def deliver(*refs):
    copies = [pltpu.make_async_copy(refs[n], refs[n + 4], refs[8].at[n]) for n in range(4)]
    for copy in copies:
        copy.start()
    for copy in copies:
        copy.wait()


def per_device(queries, keys, values, upstream, loss_mask, parents, token_count):
    any_space = pl.BlockSpec(memory_space=pl.ANY)
    hbm = pl.BlockSpec(memory_space=pltpu.HBM)
    vmem = pl.BlockSpec(memory_space=pltpu.VMEM)
    smem = pl.BlockSpec(memory_space=pltpu.SMEM)
    shapes = [(TOKENS, HEADS * SIZE)] * 2 + [(TOKENS, SIZE)] * 2
    rows = HEADS * TOKENS
    operands = [
        pltpu.with_memory_space_constraint(a, pltpu.HBM)
        for a in (queries, keys, values, upstream, loss_mask.reshape(1, TOKENS), parents)
    ]
    parts = pl.pallas_call(
        kernel,
        out_shape=[pltpu.VMEM(shape, BF16) for shape in shapes],
        in_specs=[hbm] * 4 + [any_space] * 2 + [smem],
        out_specs=[vmem] * 4,
        scratch_shapes=[
            pltpu.VMEM((TOKENS, HEADS * SIZE), BF16),
            pltpu.VMEM((2, 3 * TOKENS, SIZE), BF16),
            pltpu.VMEM((TOKENS, HEADS * SIZE), BF16),
            pltpu.VMEM((rows, SIZE), BF16),
            pltpu.VMEM((rows, SIZE), BF16),
            pltpu.VMEM((SIZE, 3 * TOKENS), BF16),
            pltpu.VMEM((3 * TOKENS, rows), BF16),
            pltpu.VMEM((2, 6, BLOCK, BLOCK), F32),
            pltpu.VMEM((8, rows), F32),
            pltpu.VMEM((3 * TOKENS, rows), BF16),
            pltpu.VMEM((2, 2, 2, BLOCK, SIZE), BF16),
            pltpu.VMEM((2, 2, 2, BLOCK, SIZE), BF16),
            pltpu.VMEM((2, TOKENS, SIZE), F32),
            pltpu.VMEM((1, TOKENS), jnp.int32),
            pltpu.SMEM((64,), jnp.int32),
            pltpu.SemaphoreType.DMA((2, PEERS)),
            pltpu.SemaphoreType.DMA((PEERS,)),
            pltpu.SemaphoreType.DMA((2, CHUNKS)),
            pltpu.SemaphoreType.DMA((2, 2)),
            pltpu.SemaphoreType.DMA((44,)),
            pltpu.SemaphoreType.DMA((PEERS, 2)),
            pltpu.SemaphoreType.DMA((6,)),
        ],
        compiler_params=pltpu.CompilerParams(
            collective_id=0, has_side_effects=True, vmem_limit_bytes=32 << 20
        ),
        cost_estimate=pl.CostEstimate(flops=5 * 10**9, bytes_accessed=3 * 10**6, transcendentals=3 * 10**6),
    )(*operands, token_count)
    return pl.pallas_call(
        deliver,
        out_shape=[jax.ShapeDtypeStruct(shape, BF16) for shape in shapes],
        in_specs=[vmem] * 4,
        out_specs=[hbm] * 4,
        scratch_shapes=[pltpu.SemaphoreType.DMA((4,))],
        compiler_params=pltpu.CompilerParams(vmem_limit_bytes=16 << 20),
    )(*parts)


def solution(mesh):
    in_specs = (
        P(("seq", "head"), None),
        P(("seq", "head"), None),
        P(("seq", "head"), None),
        P("seq", "head"),
        P("seq"),
        P(),
        P(),
    )
    out_specs = (P("seq", "head"), P("seq", "head"), P("seq", "head"), P("seq", "head"))
    return jax.shard_map(
        per_device, mesh=mesh, in_specs=in_specs, out_specs=out_specs, check_vma=False
    )
```

```python
import math

import jax
import jax.numpy as jnp
from jax import lax
from jax.experimental import pallas as pl
from jax.experimental.pallas import tpu as pltpu
from jax.sharding import PartitionSpec as P

F32 = jnp.float32
BF16 = jnp.bfloat16
TOKENS = 512
HEADS = 4
SIZE = 128
PIECE = 64
PEERS = 8
BLOCK = 256
CHUNKS = 4
CHUNK = TOKENS // CHUNKS
SCALE = 1.0 / math.sqrt(SIZE)
EXP_SCALE = math.log2(math.e) * SCALE
NEGATIVE = -1e30
SLOTS = 8
AHEAD_OWN = 8
AHEAD_GAP = 1
MESH = pl.DeviceIdType.MESH
STEPS = [(1, 0), (1, 1), (1, 3), (1, 2), (0, 1), (0, 3), (0, 2)]


def dot(a, b, left=1, right=0):
    dims = (((left,), (right,)), ((), ()))
    return lax.dot_general(a, b, dims, preferred_element_type=F32)


def ancestor_seen(parents_ref, segment):
    first = parents_ref[segment]
    second = jnp.where(first >= 0, parents_ref[jnp.maximum(first, 0)], -1)
    seen = []
    for gap in (1, 2):
        wanted = segment - gap
        seen.append((wanted >= 0) & ((first == wanted) | (second == wanted)))
    return seen


def kernel(
    q_hbm, k_hbm, v_hbm, up_hbm, mask_hbm, parents_hbm, count_ref,
    att, dq, dk_out, dv_out,
    q_in, kv, up, stacked_q, stacked_g, v_t, own_sum, stats, probs, scores, delta, dscore,
    ret_tx, ret_rx, own_grad, mask_ref, parents_ref,
    kv_sem, q_sem, gap_sem, ret_sem, send_sem, edge_sem, local_sem,
):
    segment = lax.axis_index("seq")
    group = lax.axis_index("head")
    odd = segment % 2
    sibling = segment + 1 - 2 * odd
    last = 64
    x, y = group // 4, group % 4

    my_rows = pl.ds(pl.multiple_of(group * PIECE, PIECE), PIECE)
    my_kv_cols = pl.ds(pl.multiple_of(group * SIZE, SIZE), SIZE)
    my_q_cols = pl.ds(pl.multiple_of(group * HEADS * SIZE, HEADS * SIZE), HEADS * SIZE)
    my_chunk = group // (CHUNK // PIECE)
    chip = segment // 2
    edge_source = chip // 15 - chip // 16 - chip // 30
    edge_target = chip // 16 - chip // 17
    own_copies = [
        pltpu.make_async_copy(k_hbm.at[:, my_kv_cols], kv.at[0, my_rows, :], local_sem.at[0]),
        pltpu.make_async_copy(v_hbm.at[:, my_kv_cols], kv.at[1, my_rows, :], local_sem.at[1]),
        pltpu.make_async_copy(q_hbm.at[:, my_q_cols], q_in.at[my_rows, :], local_sem.at[2]),
        pltpu.make_async_copy(up_hbm, up, local_sem.at[3]),
        pltpu.make_async_copy(mask_hbm, mask_ref, local_sem.at[4]),
        pltpu.make_async_copy(parents_hbm, parents_ref, local_sem.at[5]),
    ]
    for copy in own_copies:
        copy.start()

    barrier = pltpu.get_barrier_semaphore()
    peers = []
    for x_step, y_step in STEPS:
        peer = (x + x_step) % 2 * 4 + (y + y_step) % 4
        peers.append(peer)
        pl.semaphore_signal(barrier, inc=1, device_id={"head": peer}, device_id_type=MESH)
    pl.semaphore_signal(barrier, inc=1, device_id={"seq": sibling}, device_id_type=MESH)
    has_next = segment < last - 2
    has_before = segment >= 2


    def signal(**device):
        pl.semaphore_signal(barrier, inc=1, device_id=device, device_id_type=MESH)

    @pl.when(has_before & (edge_target == 0))
    def _():
        signal(seq=segment - 2)

    @pl.when(edge_target == 1)
    def _():
        for peer in range(PEERS):
            signal(seq=segment - 2, head=peer)

    pl.semaphore_wait(barrier, 8 + (2 * last - 3 - segment) // last + 7 * edge_source)

    sends = []

    def edge_copy(peer, i):
        cols = pl.ds(peer * SIZE, SIZE)
        return pltpu.make_async_remote_copy(
            src_ref=(k_hbm, v_hbm)[i].at[:, cols], dst_ref=kv.at[i, pl.ds(pl.multiple_of(2 * TOKENS + group * PIECE, PIECE), PIECE), :],
            send_sem=edge_sem.at[peer, i], recv_sem=gap_sem.at[1, my_chunk],
            device_id={"seq": segment + 2, "head": peer}, device_id_type=MESH,
        )

    @pl.when(edge_source == 1)
    def _():
        for peer in range(PEERS):
            for i in range(2):
                edge_copy(peer, i).start()

    def send(src, dst, recv, device):
        copy = pltpu.make_async_remote_copy(
            src_ref=src, dst_ref=dst, send_sem=send_sem.at[len(sends)], recv_sem=recv,
            device_id=device, device_id_type=MESH,
        )
        copy.start()
        sends.append(copy)

    for n, peer in enumerate(peers):
        cols = pl.ds(pl.multiple_of(peer * SIZE, SIZE), SIZE)
        send(k_hbm.at[:, cols], kv.at[0, my_rows, :], kv_sem.at[0, group], {"head": peer})
        send(v_hbm.at[:, cols], kv.at[1, my_rows, :], kv_sem.at[1, group], {"head": peer})
    for n, peer in enumerate(peers):
        cols = pl.ds(pl.multiple_of(peer * HEADS * SIZE, HEADS * SIZE), HEADS * SIZE)
        send(q_hbm.at[:, cols], q_in.at[my_rows, :], q_sem.at[group], {"head": peer})

    def wait_for(ref, sem):
        pltpu.make_async_copy(ref, ref, sem).wait()

    own_copies[0].wait()
    own_copies[1].wait()

    order = [(n + x * (CHUNKS // 2)) % CHUNKS for n in range(CHUNKS)]

    def part_of(tile, c):
        return kv.at[:, pl.ds(pl.multiple_of(tile * TOKENS + c * CHUNK, CHUNK), CHUNK), :]

    def to_next(c):
        return pltpu.make_async_remote_copy(
            src_ref=part_of(0, c), dst_ref=part_of(2, c),
            send_sem=send_sem.at[32 + c], recv_sem=gap_sem.at[1, c],
            device_id={"seq": segment + 2}, device_id_type=MESH,
        )

    def to_sibling(c, source):
        return pltpu.make_async_remote_copy(
            src_ref=part_of(source, c), dst_ref=part_of(1, c),
            send_sem=send_sem.at[36 + c], recv_sem=gap_sem.at[0, c],
            device_id={"seq": sibling}, device_id_type=MESH,
        )

    for c in order:
        for n in range(CHUNK // PIECE):
            r = c * (CHUNK // PIECE) + n
            rows = pl.ds(pl.multiple_of(r * PIECE, PIECE), PIECE)

            @pl.when(group != r)
            def _():
                wait_for(kv.at[0, rows, :], kv_sem.at[0, r])
                wait_for(kv.at[1, rows, :], kv_sem.at[1, r])

        @pl.when(has_next & (edge_source == 0))
        def _():
            to_next(c).start()

        @pl.when(odd == 0)
        def _():
            to_sibling(c, 0).start()

    def from_before():
        for c in order:

            @pl.when(has_before)
            def _():
                wait_for(part_of(2, c), gap_sem.at[1, c])

            @pl.when(has_before & (odd == 1))
            def _():
                to_sibling(c, 2).start()

    @pl.when(segment < 2)
    def _():
        kv[:, 2 * TOKENS :, :] = jnp.zeros((2, TOKENS, SIZE), BF16)

    @pl.when(segment == 0)
    def _():
        kv[:, TOKENS : 2 * TOKENS, :] = jnp.zeros((2, TOKENS, SIZE), BF16)

    own_copies[2].wait()
    for r in range(PEERS):

        @pl.when(group != r)
        def _():
            wait_for(q_in.at[pl.ds(r * PIECE, PIECE), :], q_sem.at[r])

    for h in range(HEADS):
        stacked_q[h * TOKENS : (h + 1) * TOKENS, :] = q_in[:, h * SIZE : (h + 1) * SIZE]

    for copy in own_copies[3:]:
        copy.wait()

    @pl.when(edge_target == 0)
    def _():
        from_before()

    causal = lax.broadcasted_iota(jnp.int32, (BLOCK, BLOCK), 0) <= lax.broadcasted_iota(
        jnp.int32, (BLOCK, BLOCK), 1
    )

    def column_max(s):
        return jnp.max(s.reshape(BLOCK // 8, 8, BLOCK), axis=0)

    def exponentials(slot, n, r, shift, rows, total, out):
        e = jnp.exp2(scores[slot, n] * EXP_SCALE - shift)
        part = jnp.sum(e.reshape(BLOCK // 8, 8, BLOCK), axis=0)
        total = part if total is None else total + part
        e = e.astype(BF16)
        probs[r : r + BLOCK, rows] = e
        part = dot(v_t[:, r : r + BLOCK], e)
        return total, part if out is None else out + part

    v_t[:, 0:TOKENS] = kv[1, 0:TOKENS, :].T
    def pipelined(first, second, ahead):
        steps = [(half, h) for half in range(2) for h in range(HEADS)]
        results = []
        for n in range(len(steps) + ahead):
            if n < len(steps):
                results.append(first(n % SLOTS, *steps[n]))
            if n >= ahead:
                second((n - ahead) % SLOTS, *steps[n - ahead], results[n - ahead])

    def block_rows(half, h):
        return slice(h * TOKENS + half * BLOCK, h * TOKENS + (half + 1) * BLOCK)

    def own_scores(slot, half, h):
        rows = block_rows(half, h)
        top = None
        for n in range(half + 1):
            s = dot(kv[0, n * BLOCK : (n + 1) * BLOCK, :], stacked_q[rows, :], right=1)
            if n == half:
                s = jnp.where(causal, s, NEGATIVE)
            scores[slot, n] = s
            top = column_max(s) if top is None else jnp.maximum(top, column_max(s))
        return jnp.ceil(jnp.max(top, axis=0, keepdims=True) * EXP_SCALE)

    def own_exponentials(slot, half, h, top):
        rows = block_rows(half, h)
        total, out = None, None
        for n in range(half + 1):
            total, out = exponentials(slot, n, n * BLOCK, top, rows, total, out)
        stats[0:1, rows] = top
        stats[1:2, rows] = jnp.sum(total, axis=0, keepdims=True)
        own_sum[:, rows] = out

    pipelined(own_scores, own_exponentials, AHEAD_OWN)

    @pl.when(edge_target == 1)
    def _():
        from_before()

    @pl.when(segment > 0)
    def _():
        for c in range(CHUNKS):
            wait_for(part_of(1, c), gap_sem.at[0, c])

    seen = ancestor_seen(parents_ref, segment)
    weight = mask_ref[...].astype(F32) / count_ref[0].astype(F32)

    def down(row):
        return jnp.broadcast_to(row, (SIZE, BLOCK)).T

    v_t[:, TOKENS:] = kv[1, TOKENS:, :].T
    blocks = list(range(TOKENS, 3 * TOKENS, BLOCK))

    def gap_scores(slot, half, h):
        tops = [None, None, None]
        for n, r in enumerate(blocks):
            s = dot(kv[0, r : r + BLOCK, :], stacked_q[block_rows(half, h), :], right=1)
            scores[slot, n] = s
            t = r // TOKENS
            tops[t] = column_max(s) if tops[t] is None else jnp.maximum(tops[t], column_max(s))
        top = jnp.maximum(*(jnp.where(seen[gap - 1], tops[gap], NEGATIVE) for gap in (1, 2)))
        return jnp.ceil(jnp.max(top, axis=0, keepdims=True) * EXP_SCALE)

    def gap_exponentials(slot, half, h, top):
        rows = block_rows(half, h)
        tok = slice(half * BLOCK, (half + 1) * BLOCK)
        cols = slice(h * SIZE, (h + 1) * SIZE)
        own_top = stats[0:1, rows]
        top = jnp.maximum(top, own_top)
        shifts = [None] + [jnp.where(seen[gap - 1], top, -NEGATIVE) for gap in (1, 2)]
        total, out = None, None
        for n, r in enumerate(blocks):
            total, out = exponentials(slot, n, r, shifts[r // TOKENS], rows, total, out)
        alpha = jnp.exp2(own_top - top)
        stats[2:3, rows] = alpha
        inverse = 1.0 / (jnp.sum(total, axis=0, keepdims=True) + alpha * stats[1:2, rows])
        out = ((out + alpha * own_sum[:, rows]) * inverse).T.astype(BF16)
        att[tok, cols] = out
        g = (up[tok, cols].astype(F32) * down(weight[0:1, tok] * inverse)).astype(BF16)
        stacked_g[rows, :] = g
        product = (g.astype(F32) * out.astype(F32)).T
        delta[0:1, rows] = jnp.sum(product, axis=0, keepdims=True)

    pipelined(gap_scores, gap_exponentials, AHEAD_GAP)

    def score_gradient(start, stop, rows):
        d = dot(kv[1, start:stop, :], stacked_g[rows, :], right=1) - delta[0:1, rows]
        p = probs[start:stop, rows].astype(F32)
        if start == 0:
            p = p * stats[2:3, rows]
            probs[start:stop, rows] = p.astype(BF16)
        dscore[start:stop, rows] = (p * d).astype(BF16)

    def ancestor_scores(t, half):
        start = t * TOKENS + half * BLOCK
        for n in range(2 * HEADS):
            score_gradient(start, start + BLOCK, slice(n * BLOCK, (n + 1) * BLOCK))

    def own_gradient(half):
        for h in range(HEADS):
            score_gradient(0, (half + 1) * BLOCK, block_rows(half, h))

    def ancestor_terms(t, half):
        start = t * TOKENS + half * BLOCK
        keys = slice(start, start + BLOCK)
        ret_tx[t - 1, half, 0] = (dot(dscore[keys, :], stacked_q[...]) * SCALE).astype(BF16)
        ret_tx[t - 1, half, 1] = dot(probs[keys, :], stacked_g[...]).astype(BF16)

    def part_copy(half):
        return pltpu.make_async_remote_copy(
            src_ref=ret_tx.at[0, half], dst_ref=ret_rx.at[0, half],
            send_sem=send_sem.at[40 + half], recv_sem=ret_sem.at[0, half],
            device_id={"seq": sibling}, device_id_type=MESH,
        )

    def back_copy(half):
        return pltpu.make_async_remote_copy(
            src_ref=ret_tx.at[1, half], dst_ref=ret_rx.at[1, half],
            send_sem=send_sem.at[42 + half], recv_sem=ret_sem.at[1, half],
            device_id={"seq": segment - 2}, device_id_type=MESH,
        )

    ancestor_scores(2, 0)
    ancestor_scores(2, 1)
    for half in range(2):
        if half == 1:
            ancestor_scores(1, 0)
        ancestor_terms(2, half)

        @pl.when((odd == 0) & has_before)
        def _():
            back_copy(half).start()

    ancestor_scores(1, 1)
    for half in range(2):
        if half == 1:
            own_gradient(0)
        ancestor_terms(1, half)
        part_copy(half).start()

    def join(half):
        @pl.when(odd == 1)
        def _():
            wait_for(ret_rx.at[0, half], ret_sem.at[0, half])
            ret_tx[1, half] = (ret_tx[1, half].astype(F32) + ret_rx[0, half].astype(F32)).astype(BF16)

        @pl.when((odd == 1) & has_before)
        def _():
            back_copy(half).start()

    own_gradient(1)
    own_grad[0, 0:BLOCK] = dot(dscore[0:BLOCK, :], stacked_q[...]) * SCALE
    own_grad[1, 0:BLOCK] = dot(probs[0:BLOCK, :], stacked_g[...])
    join(0)
    dk, dv = None, None
    for h in range(HEADS):
        rows = slice(h * TOKENS + BLOCK, (h + 1) * TOKENS)
        a = dot(dscore[BLOCK:TOKENS, rows], stacked_q[rows, :])
        b = dot(probs[BLOCK:TOKENS, rows], stacked_g[rows, :])
        dk = a if dk is None else dk + a
        dv = b if dv is None else dv + b
    own_grad[0, BLOCK:] = dk * SCALE
    own_grad[1, BLOCK:] = dv
    join(1)
    for half in range(2):
        own_keys = (half + 1) * BLOCK
        for h in range(HEADS):
            rows = slice(h * TOKENS + half * BLOCK, h * TOKENS + (half + 1) * BLOCK)
            total = dot(dscore[TOKENS:, rows], kv[0, TOKENS:, :], left=0) + dot(
                dscore[0:own_keys, rows], kv[0, 0:own_keys, :], left=0
            )
            tok = slice(half * BLOCK, (half + 1) * BLOCK)
            dq[tok, h * SIZE : (h + 1) * SIZE] = (total * SCALE).astype(BF16)

    @pl.when(odd == 0)
    def _():
        for half in range(2):
            wait_for(ret_rx.at[0, half], ret_sem.at[0, half])
            for i in range(2):
                rows = slice(half * BLOCK, (half + 1) * BLOCK)
                own_grad[i, rows] = own_grad[i, rows] + ret_rx[0, half, i].astype(F32)

    @pl.when(has_next)
    def _():
        for half in range(2):
            wait_for(ret_rx.at[1, half], ret_sem.at[1, half])
            for i in range(2):
                rows = slice(half * BLOCK, (half + 1) * BLOCK)
                own_grad[i, rows] = own_grad[i, rows] + ret_rx[1, half, i].astype(F32)

    dk_out[...] = own_grad[0].astype(BF16)
    dv_out[...] = own_grad[1].astype(BF16)

    for copy in sends:
        copy.wait_send()

    @pl.when(edge_source == 1)
    def _():
        for peer in range(PEERS):
            for i in range(2):
                edge_copy(peer, i).wait_send()

    for c in range(CHUNKS):

        @pl.when(has_next & (edge_source == 0))
        def _():
            to_next(c).wait_send()

        @pl.when((odd == 0) | has_before)
        def _():
            to_sibling(c, 0).wait_send()

    for half in range(2):
        part_copy(half).wait_send()

        @pl.when(has_before)
        def _():
            back_copy(half).wait_send()


def deliver(*refs):
    copies = [pltpu.make_async_copy(refs[n], refs[n + 4], refs[8].at[n]) for n in range(4)]
    for copy in copies:
        copy.start()
    for copy in copies:
        copy.wait()


def per_device(queries, keys, values, upstream, loss_mask, parents, token_count):
    any_space = pl.BlockSpec(memory_space=pl.ANY)
    hbm = pl.BlockSpec(memory_space=pltpu.HBM)
    vmem = pl.BlockSpec(memory_space=pltpu.VMEM)
    smem = pl.BlockSpec(memory_space=pltpu.SMEM)
    shapes = [(TOKENS, HEADS * SIZE)] * 2 + [(TOKENS, SIZE)] * 2
    rows = HEADS * TOKENS
    operands = [
        pltpu.with_memory_space_constraint(a, pltpu.HBM)
        for a in (queries, keys, values, upstream, loss_mask.reshape(1, TOKENS), parents)
    ]
    parts = pl.pallas_call(
        kernel,
        out_shape=[pltpu.VMEM(shape, BF16) for shape in shapes],
        in_specs=[hbm] * 4 + [any_space] * 2 + [smem],
        out_specs=[vmem] * 4,
        scratch_shapes=[
            pltpu.VMEM((TOKENS, HEADS * SIZE), BF16),
            pltpu.VMEM((2, 3 * TOKENS, SIZE), BF16),
            pltpu.VMEM((TOKENS, HEADS * SIZE), BF16),
            pltpu.VMEM((rows, SIZE), BF16),
            pltpu.VMEM((rows, SIZE), BF16),
            pltpu.VMEM((SIZE, 3 * TOKENS), BF16),
            pltpu.VMEM((SIZE, rows), F32),
            pltpu.VMEM((8, rows), F32),
            pltpu.VMEM((3 * TOKENS, rows), BF16),
            pltpu.VMEM((SLOTS, 4, BLOCK, BLOCK), F32),
            pltpu.VMEM((8, rows), F32),
            pltpu.VMEM((3 * TOKENS, rows), BF16),
            pltpu.VMEM((2, 2, 2, BLOCK, SIZE), BF16),
            pltpu.VMEM((2, 2, 2, BLOCK, SIZE), BF16),
            pltpu.VMEM((2, TOKENS, SIZE), F32),
            pltpu.VMEM((1, TOKENS), jnp.int32),
            pltpu.SMEM((64,), jnp.int32),
            pltpu.SemaphoreType.DMA((2, PEERS)),
            pltpu.SemaphoreType.DMA((PEERS,)),
            pltpu.SemaphoreType.DMA((2, CHUNKS)),
            pltpu.SemaphoreType.DMA((2, 2)),
            pltpu.SemaphoreType.DMA((44,)),
            pltpu.SemaphoreType.DMA((PEERS, 2)),
            pltpu.SemaphoreType.DMA((6,)),
        ],
        compiler_params=pltpu.CompilerParams(
            collective_id=0, has_side_effects=True, vmem_limit_bytes=32 << 20
        ),
        cost_estimate=pl.CostEstimate(flops=5 * 10**9, bytes_accessed=3 * 10**6, transcendentals=3 * 10**6),
    )(*operands, token_count)
    return pl.pallas_call(
        deliver,
        out_shape=[jax.ShapeDtypeStruct(shape, BF16) for shape in shapes],
        in_specs=[vmem] * 4,
        out_specs=[hbm] * 4,
        scratch_shapes=[pltpu.SemaphoreType.DMA((4,))],
        compiler_params=pltpu.CompilerParams(vmem_limit_bytes=16 << 20),
    )(*parts)


def solution(mesh):
    in_specs = (
        P(("seq", "head"), None),
        P(("seq", "head"), None),
        P(("seq", "head"), None),
        P("seq", "head"),
        P("seq"),
        P(),
        P(),
    )
    out_specs = (P("seq", "head"), P("seq", "head"), P("seq", "head"), P("seq", "head"))
    return jax.shard_map(
        per_device, mesh=mesh, in_specs=in_specs, out_specs=out_specs, check_vma=False
    )
```
